1024 devices in a mesh: dp: 8 (over z_hi, x), expert: 8 (over y), etp: 16 (over z_lo, core).
Axes of the slice: x: 4, y: 8, z: 16 (z_hi: 2, z_lo: 8; z = z_hi * 8 + z_lo), core: 2. Of those that a mesh axis runs over, the one named last changes fastest.
Arguments:
- grad_out: bfloat16 [4096, 6144], P(('dp', 'expert'), 'etp'), may hold values from -1.5 to 1.5
- routes: int32 [4096, 2], P(('dp', 'expert')), may hold values from 0 to 7, all different within a row; in each aligned block of 64 rows (0 to 63, 64 to 127, ...) at most 32 rows name the same one
- gate_weights: bfloat16 [4096, 2], P(('dp', 'expert')), may hold values from 0.099609375 to 1
- saved_hidden: bfloat16 [8, 8, 2, 256, 8192], P('dp', 'expert', None, None, 'etp'), may hold values from -6 to 6
- down_weight: bfloat16 [8, 8192, 6144], P('expert', 'etp'), may hold values from -0.0625 to 0.0625
Outputs:
- hidden_grad: bfloat16 [8, 8, 2, 256, 8192], P('dp', 'expert', None, None, 'etp')
- weight_grad: bfloat16 [8, 6144, 8192], P('expert', 'dp', 'etp')
The draws below stay inside these ranges and needn't reach their ends.
Inputs may be any that keep to these rules, and one draw needn't show every extreme that they name: `routes`: the two experts of a token differ; within each aligned block of 64 rows (one group) each expert is named at most 32 times.
All inputs are finite; a program needn't handle non-finite values.
Results may differ from the reference program's by a relative error of at most 0.0049.
Values may be sent and summed in bfloat16 or wider, within the bound.
A program may use at most 64 MiB of HBM per device.

```python
import math
import jax
import jax.numpy as jnp
import numpy as np
from jax import lax

D = 6144
FFW = 8192
TOP = 2
TOK = 64
EXPERTS = 8
BATCHES = 8
CAP = 32
SLOTS = 256
TOKENS = 4096


def block_levels(own_key, extent, shards, low, high):
    gain = 1.0
    for axis_at, parts in shards:
        steps = jax.random.uniform(jax.random.fold_in(jax.random.fold_in(own_key, 6), axis_at), (parts,), jnp.float32, low / len(shards), high / len(shards))
        gain = gain * jnp.repeat(jnp.exp(steps), extent[axis_at] // parts).reshape((-1,) + (1,) * (len(extent) - 1 - axis_at))
    return gain


def assign_block(rng, own, number, rows, amount, top, bound, lean):
    order = jax.random.permutation(rng, amount)
    heavy_load, ordinary = load_shares(amount, rows * top, bound, lean, True), load_shares(amount, rows * top, bound, lean, False)
    places = jnp.arange(amount)

    def named(lengths, turn):
        used = int((lengths > 0).sum())
        fixed = max(1, used // 4)
        moved = fixed + (places - fixed + turn * (used - fixed)) % max(1, amount - fixed)
        return jnp.zeros((amount,), jnp.int32).at[order[jnp.where(places < fixed, places, moved)]].set(jnp.asarray(lengths, jnp.int32))

    lengths = jnp.where(number % 4 == 0, named(heavy_load, number // 4), named(ordinary, number - number // 4 - 1))
    mixed = jax.random.permutation(jax.random.fold_in(own, 3), amount)
    source_of, sink = mixed[0:amount // 2 * 2:2], mixed[1:amount // 2 * 2:2]
    margin = jnp.minimum(lengths[source_of] - 1, bound - lengths[sink]) // 2
    margin = jnp.where((source_of == order[0]) | (sink == order[0]) | (lengths[sink] == 0), 0, jnp.maximum(margin, 0))
    moved = jax.random.randint(jax.random.fold_in(own, 4), (amount // 2,), 0, 1 << 20) % (margin + 1)
    lengths = lengths.at[source_of].add(-moved).at[sink].add(moved)
    items = jnp.searchsorted(jnp.cumsum(lengths), jnp.arange(rows * top), side="right").astype(jnp.int32)
    listing = items.reshape(top, rows).T
    listing = listing[jax.random.permutation(jax.random.fold_in(own, 1), rows)]
    turn = jax.random.randint(jax.random.fold_in(own, 2), (rows, 1), 0, top)
    return jnp.take_along_axis(listing, (jnp.arange(top)[None, :] + turn) % top, axis=1)


def load_shares(amount, total, limit, skew, full):
    portions = [(1 << 20) // math.isqrt(grade ** skew) + 1 for grade in range(1, amount + 1)]
    largest = limit if full else min(limit, max(-(-total // amount), total * portions[0] // sum(portions)))
    least = 1 if total - largest >= amount - 1 else 0
    holding, rest = [largest] + [least] * (amount - 1), total - largest - least * (amount - 1)
    while rest > 0:
        free = [i for i in range(1, amount) if holding[i] < largest] or [i for i in range(1, amount) if holding[i] < limit]
        whole, left = sum([portions[i] for i in free]), rest
        for i in free:
            more = min(limit - holding[i], max(1, left * portions[i] // whole), rest)
            holding[i] = holding[i] + more
            rest = rest - more
    return np.array(holding)


def noise(key, extent, deviation, most, split=(), held_as=jnp.bfloat16):
    result = jax.random.normal(key, extent, jnp.float32) * deviation
    if len(split) > 0:
        result = block_levels(key, extent, split, -0.22, 0.18) * result
    return jnp.clip(result, min=-most, max=most).astype(held_as)


def setup_inputs(seed: int = 0) -> dict:
    splits = jax.random.split(jax.random.key(seed), 6)
    grad_out = noise(splits[0], (TOKENS, D), 0.25, 1.5, ((0, 64), (1, 16)))
    routes_keys = jax.random.split(jax.random.fold_in(splits[1], 1), TOKENS // TOK)
    routes_turns = jax.random.permutation(jax.random.fold_in(splits[1], 3), TOKENS // TOK)
    routes = jax.vmap(lambda own, number: assign_block(jax.random.fold_in(splits[1], 2), own, number, TOK, EXPERTS, TOP, CAP, 2))(routes_keys, routes_turns).reshape((TOKENS, TOP))
    gate_weights = jnp.clip(0.099609375 + 0.9003906 * jax.random.uniform(splits[2], (TOKENS, TOP), jnp.float32) ** block_levels(splits[2], (TOKENS, TOP), ((0, 64),), -0.2, 0.2), 0.099609375, 1.0).astype(jnp.bfloat16)
    saved_hidden = noise(splits[3], (BATCHES, EXPERTS, 2, SLOTS, FFW), 1.0, 6.0, ((0, 8), (1, 8), (4, 16)))
    down_weight = noise(splits[4], (EXPERTS, FFW, D), FFW ** -0.5, 0.0625, ((0, 8), (1, 16)))
    return {"grad_out": grad_out, "routes": routes, "gate_weights": gate_weights, "saved_hidden": saved_hidden, "down_weight": down_weight}


def reference(grad_out, routes, gate_weights, saved_hidden, down_weight):
    groups = BATCHES * EXPERTS
    choices_flat = routes.reshape(groups, TOK * TOP)
    onehot = (choices_flat[:, :, None] == jnp.arange(EXPERTS, dtype=jnp.int32)[None, None, :]).astype(jnp.int32)
    order_rank = jnp.sum((jnp.cumsum(onehot, axis=1) - onehot) * onehot, axis=-1)
    group_ids = jnp.arange(groups, dtype=jnp.int32)[:, None]
    batch_idx = group_ids // EXPERTS
    source_idx = group_ids % EXPERTS
    slot_of = ((batch_idx * EXPERTS + choices_flat) * SLOTS + source_idx * CAP + order_rank).reshape(-1).astype(jnp.int32)
    rows_rep = jnp.broadcast_to(grad_out.reshape(groups, TOK, 1, D), (groups, TOK, TOP, D)).reshape(groups * TOK * TOP, D)
    dy_slots = jnp.zeros((BATCHES * EXPERTS * SLOTS, D), jnp.bfloat16).at[slot_of].set(rows_rep)
    dy_slots = dy_slots.reshape(BATCHES, EXPERTS, SLOTS, D)
    gate_slots = jnp.zeros((BATCHES * EXPERTS * SLOTS,), jnp.bfloat16).at[slot_of].set(gate_weights.reshape(-1))
    gate_slots = gate_slots.reshape(BATCHES, EXPERTS, SLOTS)
    grads_list = []
    weights_list = []
    for expert_id in range(EXPERTS):
        weight = down_weight[expert_id].astype(jnp.float32)
        rows_f32 = dy_slots[:, expert_id].astype(jnp.float32)
        raw_grad = jnp.einsum('psd,fd->psf', rows_f32, weight, precision=lax.Precision.HIGHEST)
        gate_col = gate_slots[:, expert_id].astype(jnp.float32)[:, :, None]
        gate_pre = saved_hidden[:, expert_id, 0].astype(jnp.float32)
        up_pre = saved_hidden[:, expert_id, 1].astype(jnp.float32)
        sigmoid_val = jax.nn.sigmoid(gate_pre)
        silu_val = gate_pre * sigmoid_val
        act_grad = gate_col * raw_grad
        grad_gate = act_grad * up_pre * sigmoid_val * (1.0 + gate_pre * (1.0 - sigmoid_val))
        grad_up = act_grad * silu_val
        grads_list.append(jnp.stack([grad_gate, grad_up], axis=1).astype(jnp.bfloat16))
        scaled = lax.optimization_barrier((gate_col * silu_val * up_pre).astype(jnp.bfloat16))
        scaled = scaled.astype(jnp.float32)
        summed = jnp.einsum('psd,psf->df', rows_f32, scaled, precision=lax.Precision.HIGHEST)
        weights_list.append(summed.astype(jnp.bfloat16))
    hidden_grad = jnp.stack(grads_list, axis=1)
    weight_grad = jnp.stack(weights_list, axis=0)
    return (hidden_grad, weight_grad)
```

```python
import jax
import jax.numpy as jnp
from jax import lax
from jax.experimental import pallas as pl
from jax.experimental.pallas import tpu as pltpu
from jax.sharding import PartitionSpec as P

MESH = pl.DeviceIdType.MESH
BF16 = jnp.bfloat16
F32 = jnp.float32
NE = 8
NX = 4
NZ = 8
CAP = 32
PEERS_Y = (4, 3, 5, 2, 6, 1, 7)


def kernel(
    grad_ref, routes_ref, gates_ref, saved_ref, weight_hbm, hidden_ref, wgrad_ref,
    tok, place, ranks, picked, slots, gate_out, gate_in, weight, raw, fac_gate, fac_up, act,
    scaled, far_tok, far_ranks, far_picked, rows, total,
    w_sem, gate_s, gate_r, tok_up, tok_dn, tok_r, rank_s, rank_r, far_s, far_r, pick_s, pick_r,
    sib_s, sib_r, near_s, near_r, nsib_s, nsib_r, fpick_s, fpick_r, fsib_s, fsib_r,
    cross_s, sc_s, fsc_s, sc_r,
):
    dp = lax.axis_index("dp")
    y = lax.axis_index("expert")
    etp = lax.axis_index("etp")
    half, px = lax.div(dp, NX), lax.rem(dp, NX)
    zl, core = lax.div(etp, 2), lax.rem(etp, 2)
    other = 1 - half
    tokens, width = grad_ref.shape
    nslots = NE * CAP
    mine = pl.ds(pl.multiple_of(y * CAP, CAP), CAP)

    def at(dp_=None, y_=None, z_=None, core_=None):
        return {
            "dp": dp if dp_ is None else dp_,
            "expert": y if y_ is None else y_,
            "etp": (zl if z_ is None else z_) * 2 + (core if core_ is None else core_),
        }

    def y_peer(k):
        return lax.rem(y + k, NE)

    def x_peer(k):
        return lax.rem(px + k, NX)

    def far(x):
        return at(dp_=other * NX + x)

    def near(x):
        return at(dp_=half * NX + x)

    sibling = at(core_=1 - core)

    def remote(src, dst, send, recv, where):
        return pltpu.make_async_remote_copy(
            src_ref=src, dst_ref=dst, send_sem=send, recv_sem=recv, device_id=where, device_id_type=MESH
        )

    def drain(ref, sem):
        pltpu.make_async_copy(ref, ref, sem).wait()

    barrier = pltpu.get_barrier_semaphore()

    def greet(where):
        pl.semaphore_signal(barrier, inc=1, device_id=where, device_id_type=MESH)

    for x in range(NX):
        greet(far(x))
    for k in PEERS_Y:
        greet(at(y_=y_peer(k)))
    for k in (2, 1, 3):
        greet(near(x_peer(k)))
    greet(sibling)

    @pl.when(zl > 0)
    def _():
        greet(at(z_=zl - 1))

    @pl.when(zl < NZ - 1)
    def _():
        greet(at(z_=zl + 1))

    for j in range(2 * NZ):
        pltpu.make_async_copy(weight_hbm.at[:, pl.ds(j * width, width)], weight.at[j], w_sem).start()

    lane = lax.broadcasted_iota(jnp.int32, (tokens, 128), 1)
    first = routes_ref[:, 0:1] == lane
    second = routes_ref[:, 1:2] == lane
    named = jnp.where(first | second, 1.0, 0.0).astype(BF16)
    gates = gates_ref[...].astype(F32)
    token_gate = jnp.where(first, gates[:, 0:1], 0.0) + jnp.where(second, gates[:, 1:2], 0.0)
    r_id = lax.broadcasted_iota(jnp.int32, (tokens, 128), 0)
    after = jnp.where(r_id < lane, 1.0, 0.0).astype(BF16)
    same = jnp.where(r_id == lane, 1.0, 0.0).astype(BF16)
    contract_rows = (((0,), (0,)), ((), ()))
    earlier = lax.dot_general(named, after, contract_rows, preferred_element_type=F32)
    names = lax.dot_general(named, same, contract_rows, preferred_element_type=F32)
    ranks[...] = jnp.where(names > 0.5, earlier, -1.0)[0:16].astype(BF16)

    def build_place(source):
        table = source.astype(F32)
        slot = lax.broadcasted_iota(jnp.int32, (CAP, tokens), 0).astype(F32)
        for e in range(NE):
            hit = table[e:e + 1, 0:tokens] == slot
            place[e * CAP:(e + 1) * CAP, :] = jnp.where(hit, 1.0, 0.0).astype(BF16)

    build_place(ranks[...])
    in_slots = jnp.dot(place[...], token_gate.astype(BF16), preferred_element_type=F32)
    s_row = lax.broadcasted_iota(jnp.int32, (nslots, 128), 0)
    s_lane = lax.broadcasted_iota(jnp.int32, (nslots, 128), 1)
    own_gate = jnp.where(lax.div(s_row, CAP) == s_lane, in_slots, 0.0)
    own_gate = jnp.sum(own_gate, axis=1, keepdims=True)
    gate_out[...] = jnp.broadcast_to(own_gate, (nslots, 128)).astype(BF16)
    gate_in[mine, :] = gate_out[mine, :]
    tok[zl] = grad_ref[...]

    def pick(z):
        picked[z] = jnp.dot(place[...], tok[z], preferred_element_type=F32).astype(BF16)
        slots[z, core, mine, :] = picked[z, mine, :]

    def send_picked(z):
        for k in PEERS_Y:
            to = y_peer(k)
            there = pl.ds(pl.multiple_of(to * CAP, CAP), CAP)
            remote(picked.at[z, there], slots.at[z, core, mine], pick_s.at[z], pick_r.at[z], at(y_=to)).start()

    def send_far(z):
        @pl.when(lax.div(z, NX) == other)
        def _():
            remote(tok.at[z], far_tok.at[px], far_s.at[lax.rem(z, NX)], far_r.at[px], far(lax.rem(z, NX))).start()

    pick(zl)

    ends = jnp.where(zl > 0, 1, 0) + jnp.where(zl < NZ - 1, 1, 0)
    pl.semaphore_wait(barrier, 15 + ends)

    for k in PEERS_Y:
        to = y_peer(k)
        there = pl.ds(pl.multiple_of(to * CAP, CAP), CAP)
        remote(gate_out.at[there], gate_in.at[mine], gate_s, gate_r, at(y_=to)).start()

    @pl.when(zl < NZ - 1)
    def _():
        remote(tok.at[zl], tok.at[zl], tok_up.at[zl], tok_r.at[zl], at(z_=zl + 1)).start()

    @pl.when(zl > 0)
    def _():
        remote(tok.at[zl], tok.at[zl], tok_dn.at[zl], tok_r.at[zl], at(z_=zl - 1)).start()

    for x in range(NX):
        remote(ranks, far_ranks.at[px], rank_s.at[x], rank_r.at[px], far(x)).start()
    send_far(zl)
    send_picked(zl)

    gate_pre = saved_ref[0].astype(F32)
    up_pre = saved_ref[1].astype(F32)
    sig = jax.nn.sigmoid(gate_pre)
    silu = gate_pre * sig
    fac_gate[...] = up_pre * sig * (1.0 + gate_pre * (1.0 - sig))
    fac_up[...] = silu
    act[...] = silu * up_pre

    def nearest(k):
        short = jnp.minimum(zl, NZ - 1 - zl)
        step = lax.div(k + 1, 2)
        zigzag = jnp.where(lax.rem(k, 2) == 1, zl - step, zl + step)
        return jnp.where(k <= 2 * short, zigzag, jnp.where(zl < NZ // 2, k, NZ - 1 - k))

    def pass_tokens(k, carry):
        z = nearest(k)
        drain(tok.at[z], tok_r.at[z])

        @pl.when((z < zl) & (zl < NZ - 1))
        def _():
            remote(tok.at[z], tok.at[z], tok_up.at[z], tok_r.at[z], at(z_=zl + 1)).start()

        @pl.when((z > zl) & (zl > 0))
        def _():
            remote(tok.at[z], tok.at[z], tok_dn.at[z], tok_r.at[z], at(z_=zl - 1)).start()

        send_far(z)
        pick(z)
        send_picked(z)
        return carry

    lax.fori_loop(1, 4, pass_tokens, 0)

    drain(gate_in.at[0:nslots - CAP], gate_r)
    gate_col = gate_in[...].astype(F32)[:, 0:1]
    scaled[dp] = (gate_col * act[...]).astype(BF16)
    hrows = nslots // 2
    for h in range(2):
        part = scaled.at[dp, pl.ds(h * hrows, hrows)]
        remote(part, part, cross_s.at[h], sc_r.at[dp, h], far(px)).start()
    for k in (2, 1, 3):
        x = x_peer(k)
        for h in range(2):
            part = scaled.at[dp, pl.ds(h * hrows, hrows)]
            remote(part, part, sc_s.at[h, x], sc_r.at[dp, h], near(x)).start()

    lax.fori_loop(4, NZ, pass_tokens, 0)

    drain(weight, w_sem)
    raw[...] = jnp.zeros_like(raw)
    total[...] = jnp.zeros_like(total)

    def add_raw(z, c):
        raw[...] += lax.dot_general(
            slots[z, c], weight[2 * z + c], (((1,), (1,)), ((), ())), preferred_element_type=F32
        )

    def take_slots(k, carry):
        z = nearest(k)
        drain(slots.at[z, core, pl.ds(0, nslots - CAP)], pick_r.at[z])
        block = slots.at[z, core]
        remote(block, block, sib_s.at[z], sib_r.at[z], sibling).start()

        @pl.when((lax.div(z, NX) == half) & (z != dp))
        def _():
            x = lax.rem(z, NX)
            remote(block, rows.at[dp, core], near_s.at[x], near_r.at[px], near(x)).start()

        add_raw(z, core)

        @pl.when(k > 0)
        def _():
            before = nearest(jnp.maximum(k - 1, 0))
            drain(slots.at[before, 1 - core], sib_r.at[before])
            add_raw(before, 1 - core)

        return carry

    lax.fori_loop(0, 4, take_slots, 0)

    def take_far(q, carry):
        drain(far_ranks.at[q], rank_r.at[q])
        drain(far_tok.at[q], far_r.at[q])
        build_place(far_ranks[q])
        far_picked[q] = jnp.dot(place[...], far_tok[q], preferred_element_type=F32).astype(BF16)
        far_dp = other * NX + q
        rows[far_dp, core, mine, :] = far_picked[q, mine, :]
        for k in PEERS_Y:
            to = y_peer(k)
            there = pl.ds(pl.multiple_of(to * CAP, CAP), CAP)
            remote(
                far_picked.at[q, there], rows.at[far_dp, core, mine], fpick_s.at[q], fpick_r.at[q], at(y_=to)
            ).start()
        return carry

    lax.fori_loop(0, NX, take_far, 0)
    lax.fori_loop(4, 6, take_slots, 0)

    twin = other * NX + px
    for h in range(2):
        part = scaled.at[twin, pl.ds(h * hrows, hrows)]
        drain(part, sc_r.at[twin, h])
        for k in (2, 1, 3):
            x = x_peer(k)
            remote(part, part, fsc_s.at[h, x], sc_r.at[twin, h], near(x)).start()

    lax.fori_loop(6, NZ, take_slots, 0)
    last = nearest(NZ - 1)
    drain(slots.at[last, 1 - core], sib_r.at[last])
    add_raw(last, 1 - core)
    gated = gate_in[...].astype(F32)[:, 0:1] * raw[...]
    hidden_ref[0] = (gated * fac_gate[...]).astype(BF16)
    hidden_ref[1] = (gated * fac_up[...]).astype(BF16)

    def add_total(c, left, right):
        total[c] += lax.dot_general(left, right, contract_rows, preferred_element_type=F32)

    for c in range(2):
        add_total(c, slots[dp, c], scaled[dp])

    def near_arrive(k, carry):
        x = x_peer(k)
        src = half * NX + x
        block = rows.at[src, core]
        drain(block, near_r.at[x])
        remote(block, block, nsib_s.at[x], nsib_r.at[x], sibling).start()
        return carry

    lax.fori_loop(1, NX, near_arrive, 0)

    def near_add(k, carry):
        x = x_peer(k)
        src = half * NX + x
        for h in range(2):
            drain(scaled.at[src, pl.ds(h * hrows, hrows)], sc_r.at[src, h])
        add_total(core, rows[src, core], scaled[src])
        drain(rows.at[src, 1 - core], nsib_r.at[x])
        add_total(1 - core, rows[src, 1 - core], scaled[src])
        return carry

    lax.fori_loop(1, NX, near_add, 0)

    def far_arrive(q, carry):
        src = other * NX + q
        drain(rows.at[src, core, pl.ds(0, nslots - CAP)], fpick_r.at[q])
        block = rows.at[src, core]
        remote(block, block, fsib_s.at[q], fsib_r.at[q], sibling).start()

        @pl.when(q != px)
        def _():
            for h in range(2):
                drain(scaled.at[src, pl.ds(h * hrows, hrows)], sc_r.at[src, h])

        add_total(core, rows[src, core], scaled[src])
        drain(rows.at[src, 1 - core], fsib_r.at[q])
        add_total(1 - core, rows[src, 1 - core], scaled[src])
        return carry

    lax.fori_loop(0, NX, far_arrive, 0)
    wgrad_ref[0:width, :] = total[0].astype(BF16)
    wgrad_ref[width:2 * width, :] = total[1].astype(BF16)

    drain(gate_out.at[0:nslots - CAP], gate_s)
    for x in range(NX):
        drain(ranks, rank_s.at[x])

    def sent_blocks(z, carry):
        @pl.when((z <= zl) & (zl < NZ - 1))
        def _():
            drain(tok.at[z], tok_up.at[z])

        @pl.when((z >= zl) & (zl > 0))
        def _():
            drain(tok.at[z], tok_dn.at[z])

        drain(picked.at[z, pl.ds(0, nslots - CAP)], pick_s.at[z])
        drain(slots.at[z, core], sib_s.at[z])
        return carry

    lax.fori_loop(0, NZ, sent_blocks, 0)

    def sent_parts(q, carry):
        drain(tok.at[0], far_s.at[q])
        drain(far_picked.at[q, pl.ds(0, nslots - CAP)], fpick_s.at[q])
        drain(rows.at[q, core], fsib_s.at[q])

        @pl.when(q != px)
        def _():
            drain(rows.at[q, core], near_s.at[q])
            drain(rows.at[q, core], nsib_s.at[q])
            for h in range(2):
                drain(scaled.at[q, pl.ds(0, hrows)], sc_s.at[h, q])
                drain(scaled.at[q, pl.ds(0, hrows)], fsc_s.at[h, q])

        return carry

    lax.fori_loop(0, NX, sent_parts, 0)
    for h in range(2):
        drain(scaled.at[dp, pl.ds(0, hrows)], cross_s.at[h])


def per_device(grad_out, routes, gate_weights, saved_hidden, down_weight):
    tokens, width = grad_out.shape
    nslots, units = saved_hidden.shape[3:]
    dma = pltpu.SemaphoreType.DMA
    vmem = pl.BlockSpec(memory_space=pltpu.VMEM)
    hidden_grad, weight_grad = pl.pallas_call(
        kernel,
        out_shape=(
            jax.ShapeDtypeStruct((2, nslots, units), BF16),
            jax.ShapeDtypeStruct((2 * width, units), BF16),
        ),
        in_specs=[vmem, vmem, vmem, vmem, pl.BlockSpec(memory_space=pl.ANY)],
        out_specs=(vmem, vmem),
        scratch_shapes=[
            pltpu.VMEM((NZ, tokens, width), BF16),
            pltpu.VMEM((nslots, tokens), BF16),
            pltpu.VMEM((16, 128), BF16),
            pltpu.VMEM((NZ, nslots, width), BF16),
            pltpu.VMEM((NZ, 2, nslots, width), BF16),
            pltpu.VMEM((nslots, 128), BF16),
            pltpu.VMEM((nslots, 128), BF16),
            pltpu.VMEM((2 * NZ, units, width), BF16),
            pltpu.VMEM((nslots, units), F32),
            pltpu.VMEM((nslots, units), F32),
            pltpu.VMEM((nslots, units), F32),
            pltpu.VMEM((nslots, units), F32),
            pltpu.VMEM((2 * NX, nslots, units), BF16),
            pltpu.VMEM((NX, tokens, width), BF16),
            pltpu.VMEM((NX, 16, 128), BF16),
            pltpu.VMEM((NX, nslots, width), BF16),
            pltpu.VMEM((2 * NX, 2, nslots, width), BF16),
            pltpu.VMEM((2, width, units), F32),
            dma(()),
            dma(()), dma(()),
            dma((NZ,)), dma((NZ,)), dma((NZ,)),
            dma((NX,)), dma((NX,)),
            dma((NX,)), dma((NX,)),
            dma((NZ,)), dma((NZ,)),
            dma((NZ,)), dma((NZ,)),
            dma((NX,)), dma((NX,)),
            dma((NX,)), dma((NX,)),
            dma((NX,)), dma((NX,)),
            dma((NX,)), dma((NX,)),
            dma((2,)), dma((2, NX)), dma((2, NX)), dma((2 * NX, 2)),
        ],
        compiler_params=pltpu.CompilerParams(
            collective_id=0, has_side_effects=True, vmem_limit_bytes=56 * 2**20
        ),
        name="moe_backward",
    )(grad_out, routes, gate_weights, saved_hidden[0, 0], down_weight[0])
    return hidden_grad[None, None], weight_grad[None]


def solution(mesh):
    placed = (
        P(("dp", "expert"), "etp"),
        P(("dp", "expert"), None),
        P(("dp", "expert"), None),
        P("dp", "expert", None, None, "etp"),
        P("expert", "etp", None),
    )
    return jax.shard_map(
        per_device,
        mesh=mesh,
        in_specs=placed,
        out_specs=(P("dp", "expert", None, None, "etp"), P("expert", "dp", "etp")),
        check_vma=False,
    )
```

```python
import jax
import jax.numpy as jnp
from jax import lax
from jax.experimental import pallas as pl
from jax.experimental.pallas import tpu as pltpu
from jax.sharding import PartitionSpec as P

MESH = pl.DeviceIdType.MESH
BF16 = jnp.bfloat16
F32 = jnp.float32
NE = 8
NX = 4
NZ = 8
CAP = 32
PARTS = 8
FIRST = 3
PEERS_Y = (4, 3, 5, 2, 6, 1, 7)


def kernel(
    grad_ref, routes_ref, gates_ref, saved_ref, weight_hbm, hidden_ref, wgrad_ref,
    tok, place, far_src, picked, slots, gate_out, gate_in, weight, raw, fac_gate, fac_up, act,
    scaled, far_tok, far_picked, rows, total,
    w_sem, gate_s, gate_r, tok_up, tok_dn, tok_r, far_s, far_r, far_up, far_dn, pick_s, pick_r,
    sib_s, sib_r, near_s, near_r, nsib_s, nsib_r, fpick_s, fpick_r, fsib_s, fsib_r,
    cross_s, cross_r, sc_s, sc_r, fsc_s, fsc_r,
):
    dp = lax.axis_index("dp")
    y = lax.axis_index("expert")
    etp = lax.axis_index("etp")
    half, px = lax.div(dp, NX), lax.rem(dp, NX)
    zl, core = lax.div(etp, 2), lax.rem(etp, 2)
    other = 1 - half
    tokens, width = grad_ref.shape
    nslots = NE * CAP
    mine = pl.ds(pl.multiple_of(y * CAP, CAP), CAP)

    def at(dp_=None, y_=None, z_=None, core_=None):
        return {
            "dp": dp if dp_ is None else dp_,
            "expert": y if y_ is None else y_,
            "etp": (zl if z_ is None else z_) * 2 + (core if core_ is None else core_),
        }

    def y_peer(k):
        return lax.rem(y + k, NE)

    def x_peer(k):
        return lax.rem(px + k, NX)

    def far(x):
        return at(dp_=other * NX + x)

    def near(x):
        return at(dp_=half * NX + x)

    sibling = at(core_=1 - core)

    def remote(src, dst, send, recv, where):
        return pltpu.make_async_remote_copy(
            src_ref=src, dst_ref=dst, send_sem=send, recv_sem=recv, device_id=where, device_id_type=MESH
        )

    def drain(ref, sem):
        pltpu.make_async_copy(ref, ref, sem).wait()

    barrier = pltpu.get_barrier_semaphore()

    def greet(where):
        pl.semaphore_signal(barrier, inc=1, device_id=where, device_id_type=MESH)

    far_source = lax.div(zl, NX) == other
    far_target = zl == jnp.where(half == 0, NZ // 2, NZ // 2 - 1)
    far_above = zl >= jnp.where(half == 0, NZ // 2, NZ // 2 - 1)
    far_below = zl <= jnp.where(half == 0, NZ // 2, NZ // 2 - 1)

    @pl.when(far_target)
    def _():
        for x in range(NX):
            greet(at(dp_=other * NX + x, z_=dp))

    greet(far(px))
    for k in PEERS_Y:
        greet(at(y_=y_peer(k)))
    for k in (2, 1, 3):
        greet(near(x_peer(k)))
    greet(sibling)

    @pl.when(zl > 0)
    def _():
        greet(at(z_=zl - 1))

    @pl.when(zl < NZ - 1)
    def _():
        greet(at(z_=zl + 1))

    for j in range(2 * NZ):
        pltpu.make_async_copy(weight_hbm.at[:, pl.ds(j * width, width)], weight.at[j], w_sem).start()

    contract_rows = (((0,), (0,)), ((), ()))

    expert_id = lax.broadcasted_iota(jnp.int32, (16, tokens), 0)
    first = routes_ref[0:1, :] == expert_id
    second = routes_ref[1:2, :] == expert_id
    named = jnp.where(first | second, 1.0, 0.0)
    gates = gates_ref[...].astype(F32)
    token_gate = jnp.where(first, gates[0:1, :], 0.0) + jnp.where(second, gates[1:2, :], 0.0)
    row = lax.broadcasted_iota(jnp.int32, (tokens, tokens), 0)
    col = lax.broadcasted_iota(jnp.int32, (tokens, tokens), 1)
    after = jnp.where(row < col, 1.0, 0.0).astype(BF16)
    earlier = jnp.dot(named.astype(BF16), after, preferred_element_type=F32)
    table = jnp.where(named > 0.5, earlier, -1.0)
    slot = lax.broadcasted_iota(jnp.int32, (CAP, tokens), 0).astype(F32)

    def build_place(table):
        for e in range(NE):
            hit = jnp.where(table[e:e + 1, :] == slot, 1.0, 0.0)
            place[e * CAP:(e + 1) * CAP, :] = hit.astype(BF16)

    for e in range(NE):
        hit = jnp.where(table[e:e + 1, :] == slot, 1.0, 0.0)
        place[e * CAP:(e + 1) * CAP, :] = hit.astype(BF16)
        gate = jnp.sum(hit * token_gate[e:e + 1, :], axis=1, keepdims=True)
        gate_out[e * CAP:(e + 1) * CAP, :] = jnp.broadcast_to(gate, (CAP, 128)).astype(BF16)

    gate_in[mine, :] = gate_out[mine, :]
    tok[zl] = grad_ref[...]
    far_src[0:tokens, :] = grad_ref[...]
    far_src[tokens:tokens + 16, 0:tokens] = table.astype(BF16)

    def pick(z):
        picked[z] = jnp.dot(place[...], tok[z], preferred_element_type=F32).astype(BF16)
        slots[z, core, mine, :] = picked[z, mine, :]

    def send_picked(z):
        for k in PEERS_Y:
            to = y_peer(k)
            there = pl.ds(pl.multiple_of(to * CAP, CAP), CAP)
            remote(picked.at[z, there], slots.at[z, core, mine], pick_s.at[z], pick_r.at[z], at(y_=to)).start()

    pick(zl)

    ends = jnp.where(zl > 0, 1, 0) + jnp.where(zl < NZ - 1, 1, 0)
    pl.semaphore_wait(barrier, 12 + ends + jnp.where(far_source, 1, 0))

    for k in PEERS_Y:
        to = y_peer(k)
        there = pl.ds(pl.multiple_of(to * CAP, CAP), CAP)
        remote(gate_out.at[there], gate_in.at[mine], gate_s, gate_r, at(y_=to)).start()

    @pl.when(zl < NZ - 1)
    def _():
        remote(tok.at[zl], tok.at[zl], tok_up.at[zl], tok_r.at[zl], at(z_=zl + 1)).start()

    @pl.when(zl > 0)
    def _():
        remote(tok.at[zl], tok.at[zl], tok_dn.at[zl], tok_r.at[zl], at(z_=zl - 1)).start()

    @pl.when(far_source)
    def _():
        land = jnp.where(other == 0, NZ // 2, NZ // 2 - 1)
        remote(far_src, far_tok.at[px], far_s, far_r.at[px], at(dp_=zl, z_=land)).start()

    send_picked(zl)

    gate_pre = saved_ref[0].astype(F32)
    up_pre = saved_ref[1].astype(F32)
    sig = jax.nn.sigmoid(gate_pre)
    silu = gate_pre * sig
    fac_gate[...] = up_pre * sig * (1.0 + gate_pre * (1.0 - sig))
    fac_up[...] = silu
    act[...] = silu * up_pre

    def nearest(k):
        short = jnp.minimum(zl, NZ - 1 - zl)
        step = lax.div(k + 1, 2)
        zigzag = jnp.where(lax.rem(k, 2) == 1, zl - step, zl + step)
        return jnp.where(k <= 2 * short, zigzag, jnp.where(zl < NZ // 2, k, NZ - 1 - k))

    def pass_far(q, carry):
        block = far_tok.at[q]
        drain(block, far_r.at[q])

        @pl.when(far_above & (zl < NZ - 1))
        def _():
            remote(block, block, far_up.at[q], far_r.at[q], at(z_=zl + 1)).start()

        @pl.when(far_below & (zl > 0))
        def _():
            remote(block, block, far_dn.at[q], far_r.at[q], at(z_=zl - 1)).start()

        return carry

    part_rows = nslots // PARTS

    def part_of(where, h):
        return scaled.at[where, pl.ds(pl.multiple_of(h * part_rows, part_rows), part_rows)]

    def start_cross(h):
        remote(part_of(dp, h), part_of(dp, h), cross_s.at[h], cross_r.at[h], far(px)).start()

    far_step = 2 + jnp.abs(zl - jnp.where(half == 0, NZ // 2, NZ // 2 - 1))

    def pass_tokens(t, carry):
        below, above = zl - t, zl + t

        @pl.when(below >= 0)
        def _():
            block = tok.at[below]
            drain(block, tok_r.at[below])

            @pl.when(zl < NZ - 1)
            def _():
                remote(block, block, tok_up.at[below], tok_r.at[below], at(z_=zl + 1)).start()

        @pl.when(above < NZ)
        def _():
            block = tok.at[above]
            drain(block, tok_r.at[above])

            @pl.when(zl > 0)
            def _():
                remote(block, block, tok_dn.at[above], tok_r.at[above], at(z_=zl - 1)).start()

        @pl.when(below >= 0)
        def _():
            pick(below)
            send_picked(below)

        @pl.when(above < NZ)
        def _():
            pick(above)
            send_picked(above)

        @pl.when(t >= FIRST)
        def _():
            start_cross(t - FIRST)

        @pl.when(t == far_step)
        def _():
            lax.fori_loop(0, NX, pass_far, 0)

        return carry

    lax.fori_loop(1, FIRST, pass_tokens, 0)

    drain(gate_in.at[0:nslots - CAP], gate_r)
    gate_col = gate_in[...].astype(F32)[:, 0:1]
    scaled[dp] = (gate_col * act[...]).astype(BF16)
    for k in (2, 1, 3):
        x = x_peer(k)
        remote(scaled.at[dp], scaled.at[dp], sc_s.at[x], sc_r.at[px], near(x)).start()

    lax.fori_loop(FIRST, NZ, pass_tokens, 0)
    for h in range(NZ - FIRST, PARTS):
        start_cross(h)

    drain(weight, w_sem)
    raw[...] = jnp.zeros_like(raw)
    total[...] = jnp.zeros_like(total)

    def add_raw(z, c):
        raw[...] += lax.dot_general(
            slots[z, c], weight[2 * z + c], (((1,), (1,)), ((), ())), preferred_element_type=F32
        )

    def take_slots(k, carry):
        z = nearest(k)
        drain(slots.at[z, core, pl.ds(0, nslots - CAP)], pick_r.at[z])
        block = slots.at[z, core]
        remote(block, block, sib_s.at[z], sib_r.at[z], sibling).start()

        @pl.when((lax.div(z, NX) == half) & (z != dp))
        def _():
            x = lax.rem(z, NX)
            remote(block, rows.at[dp, core], near_s.at[x], near_r.at[px], near(x)).start()

        add_raw(z, core)

        @pl.when(k > 0)
        def _():
            before = nearest(jnp.maximum(k - 1, 0))
            drain(slots.at[before, 1 - core], sib_r.at[before])
            add_raw(before, 1 - core)

        return carry

    def take_far(q, carry):
        build_place(far_tok[q, tokens:tokens + 16, 0:tokens].astype(F32))
        far_picked[q] = jnp.dot(
            place[...], far_tok[q, 0:tokens, :], preferred_element_type=F32
        ).astype(BF16)
        far_dp = other * NX + q
        rows[far_dp, core, mine, :] = far_picked[q, mine, :]
        for k in PEERS_Y:
            to = y_peer(k)
            there = pl.ds(pl.multiple_of(to * CAP, CAP), CAP)
            remote(
                far_picked.at[q, there], rows.at[far_dp, core, mine], fpick_s.at[q], fpick_r.at[q], at(y_=to)
            ).start()
        return carry

    lax.fori_loop(0, NX, take_far, 0)
    lax.fori_loop(0, 6, take_slots, 0)

    twin = other * NX + px

    def pass_part(h):
        part = scaled.at[twin, pl.ds(2 * h * part_rows, 2 * part_rows)]
        for i in range(2):
            drain(part_of(twin, 2 * h + i), cross_r.at[2 * h + i])
        for k in (2, 1, 3):
            x = x_peer(k)
            remote(part, part, fsc_s.at[x], fsc_r.at[px], near(x)).start()

    pass_part(0)
    take_slots(6, 0)
    pass_part(1)
    take_slots(7, 0)
    pass_part(2)
    last = nearest(NZ - 1)
    drain(slots.at[last, 1 - core], sib_r.at[last])
    add_raw(last, 1 - core)
    gated = gate_in[...].astype(F32)[:, 0:1] * raw[...]
    hidden_ref[0] = (gated * fac_gate[...]).astype(BF16)
    hidden_ref[1] = (gated * fac_up[...]).astype(BF16)

    def add_total(c, left, right):
        total[c] += lax.dot_general(left, right, contract_rows, preferred_element_type=F32)

    for c in range(2):
        add_total(c, slots[dp, c], scaled[dp])

    def near_arrive(k, carry):
        x = x_peer(k)
        src = half * NX + x
        block = rows.at[src, core]
        drain(block, near_r.at[x])
        remote(block, block, nsib_s.at[x], nsib_r.at[x], sibling).start()
        return carry

    lax.fori_loop(1, NX, near_arrive, 0)

    def near_add(k, carry):
        x = x_peer(k)
        src = half * NX + x
        drain(scaled.at[src], sc_r.at[x])
        add_total(core, rows[src, core], scaled[src])
        drain(rows.at[src, 1 - core], nsib_r.at[x])
        add_total(1 - core, rows[src, 1 - core], scaled[src])
        return carry

    lax.fori_loop(1, NX, near_add, 0)

    pass_part(3)

    def far_arrive(q, carry):
        src = other * NX + q
        drain(rows.at[src, core, pl.ds(0, nslots - CAP)], fpick_r.at[q])
        block = rows.at[src, core]
        remote(block, block, fsib_s.at[q], fsib_r.at[q], sibling).start()
        return carry

    def far_add(q, carry):
        src = other * NX + q

        @pl.when(q != px)
        def _():
            drain(scaled.at[src], fsc_r.at[q])

        add_total(core, rows[src, core], scaled[src])
        drain(rows.at[src, 1 - core], fsib_r.at[q])
        add_total(1 - core, rows[src, 1 - core], scaled[src])
        return carry

    lax.fori_loop(0, NX, far_arrive, 0)
    lax.fori_loop(0, NX, far_add, 0)
    wgrad_ref[0:width, :] = total[0].astype(BF16)
    wgrad_ref[width:2 * width, :] = total[1].astype(BF16)

    drain(gate_out.at[0:nslots - CAP], gate_s)

    @pl.when(far_source)
    def _():
        drain(far_src, far_s)

    def sent_blocks(z, carry):
        @pl.when((z <= zl) & (zl < NZ - 1))
        def _():
            drain(tok.at[z], tok_up.at[z])

        @pl.when((z >= zl) & (zl > 0))
        def _():
            drain(tok.at[z], tok_dn.at[z])

        drain(picked.at[z, pl.ds(0, nslots - CAP)], pick_s.at[z])
        drain(slots.at[z, core], sib_s.at[z])
        return carry

    lax.fori_loop(0, NZ, sent_blocks, 0)

    def sent_parts(q, carry):
        @pl.when(far_above & (zl < NZ - 1))
        def _():
            drain(far_tok.at[q], far_up.at[q])

        @pl.when(far_below & (zl > 0))
        def _():
            drain(far_tok.at[q], far_dn.at[q])

        drain(far_picked.at[q, pl.ds(0, nslots - CAP)], fpick_s.at[q])
        drain(rows.at[q, core], fsib_s.at[q])

        @pl.when(q != px)
        def _():
            drain(rows.at[q, core], near_s.at[q])
            drain(rows.at[q, core], nsib_s.at[q])
            drain(scaled.at[q], sc_s.at[q])
            drain(scaled.at[q], fsc_s.at[q])

        return carry

    lax.fori_loop(0, NX, sent_parts, 0)
    for h in range(PARTS):
        drain(part_of(dp, h), cross_s.at[h])


def hand_over(hidden_in, wgrad_in, hidden_out, wgrad_out):
    hidden_out[...] = hidden_in[...]
    wgrad_out[...] = wgrad_in[...]


def per_device(grad_out, routes, gate_weights, saved_hidden, down_weight):
    tokens, width = grad_out.shape
    nslots, units = saved_hidden.shape[3:]
    dma = pltpu.SemaphoreType.DMA
    vmem = pl.BlockSpec(memory_space=pltpu.VMEM)
    hidden_grad, weight_grad = pl.pallas_call(
        kernel,
        out_shape=(
            jax.ShapeDtypeStruct((2, nslots, units), BF16),
            jax.ShapeDtypeStruct((2 * width, units), BF16),
        ),
        in_specs=[vmem, vmem, vmem, vmem, pl.BlockSpec(memory_space=pl.ANY)],
        out_specs=(vmem, vmem),
        scratch_shapes=[
            pltpu.VMEM((NZ, tokens, width), BF16),
            pltpu.VMEM((nslots, tokens), BF16),
            pltpu.VMEM((tokens + 16, width), BF16),
            pltpu.VMEM((NZ, nslots, width), BF16),
            pltpu.VMEM((NZ, 2, nslots, width), BF16),
            pltpu.VMEM((nslots, 128), BF16),
            pltpu.VMEM((nslots, 128), BF16),
            pltpu.VMEM((2 * NZ, units, width), BF16),
            pltpu.VMEM((nslots, units), F32),
            pltpu.VMEM((nslots, units), F32),
            pltpu.VMEM((nslots, units), F32),
            pltpu.VMEM((nslots, units), F32),
            pltpu.VMEM((2 * NX, nslots, units), BF16),
            pltpu.VMEM((NX, tokens + 16, width), BF16),
            pltpu.VMEM((NX, nslots, width), BF16),
            pltpu.VMEM((2 * NX, 2, nslots, width), BF16),
            pltpu.VMEM((2, width, units), F32),
            dma(()),
            dma(()), dma(()),
            dma((NZ,)), dma((NZ,)), dma((NZ,)),
            dma(()), dma((NX,)), dma((NX,)), dma((NX,)),
            dma((NZ,)), dma((NZ,)),
            dma((NZ,)), dma((NZ,)),
            dma((NX,)), dma((NX,)),
            dma((NX,)), dma((NX,)),
            dma((NX,)), dma((NX,)),
            dma((NX,)), dma((NX,)),
            dma((PARTS,)), dma((PARTS,)),
            dma((NX,)), dma((NX,)), dma((NX,)), dma((NX,)),
        ],
        compiler_params=pltpu.CompilerParams(
            collective_id=0, has_side_effects=True, vmem_limit_bytes=56 * 2**20
        ),
        name="moe_backward",
    )(grad_out, routes.T, gate_weights.T, saved_hidden[0, 0], down_weight[0])
    hidden_grad, weight_grad = pl.pallas_call(
        hand_over,
        out_shape=(
            jax.ShapeDtypeStruct(hidden_grad.shape, BF16),
            jax.ShapeDtypeStruct(weight_grad.shape, BF16),
        ),
        in_specs=[vmem, vmem],
        out_specs=(vmem, vmem),
        name="hand_over",
    )(hidden_grad, weight_grad)
    return hidden_grad[None, None], weight_grad[None]


def solution(mesh):
    placed = (
        P(("dp", "expert"), "etp"),
        P(("dp", "expert"), None),
        P(("dp", "expert"), None),
        P("dp", "expert", None, None, "etp"),
        P("expert", "etp", None),
    )
    return jax.shard_map(
        per_device,
        mesh=mesh,
        in_specs=placed,
        out_specs=(P("dp", "expert", None, None, "etp"), P("expert", "dp", "etp")),
        check_vma=False,
    )
```

```python
import jax
import jax.numpy as jnp
from jax import lax
from jax.experimental import pallas as pl
from jax.experimental.pallas import tpu as pltpu
from jax.sharding import PartitionSpec as P

MESH = pl.DeviceIdType.MESH
BF16 = jnp.bfloat16
F32 = jnp.float32
NE = 8
NX = 4
NZ = 8
CAP = 32
PARTS = 4
PEERS_Y = (4, 3, 5, 2, 6, 1, 7)


def kernel(
    grad_ref, routes_ref, gates_ref, saved_ref, weight_hbm, hidden_ref, wgrad_ref,
    tok, place, far_src, picked, slots, gate_out, gate_in, weight, raw, fac_gate, fac_up, act,
    scaled, hop, far_tok, far_picked, rows, total,
    w_sem, gate_s, gate_r, tok_up, tok_dn, tok_r, far_s, far_r, far_up, far_dn, pick_s, pick_r,
    sib_s, sib_r, near_s, near_r, nsib_s, nsib_r, fpick_s, fpick_r, fsib_s, fsib_r,
    hop_s, hop_r, sc_s, sc_r, fsc_s, fsc_r,
):
    dp = lax.axis_index("dp")
    y = lax.axis_index("expert")
    etp = lax.axis_index("etp")
    half, px = lax.div(dp, NX), lax.rem(dp, NX)
    zl, core = lax.div(etp, 2), lax.rem(etp, 2)
    other = 1 - half
    tokens, width = grad_ref.shape
    nslots = NE * CAP
    mine = pl.ds(pl.multiple_of(y * CAP, CAP), CAP)

    def at(dp_=None, y_=None, z_=None, core_=None):
        return {
            "dp": dp if dp_ is None else dp_,
            "expert": y if y_ is None else y_,
            "etp": (zl if z_ is None else z_) * 2 + (core if core_ is None else core_),
        }

    def y_peer(k):
        return lax.rem(y + k, NE)

    def x_peer(k):
        return lax.rem(px + k, NX)

    def near(x):
        return at(dp_=half * NX + x)

    sibling = at(core_=1 - core)

    def remote(src, dst, send, recv, where):
        return pltpu.make_async_remote_copy(
            src_ref=src, dst_ref=dst, send_sem=send, recv_sem=recv, device_id=where, device_id_type=MESH
        )

    def drain(ref, sem):
        pltpu.make_async_copy(ref, ref, sem).wait()

    barrier = pltpu.get_barrier_semaphore()

    def greet(where):
        pl.semaphore_signal(barrier, inc=1, device_id=where, device_id_type=MESH)

    far_source = lax.div(zl, NX) == other
    far_target = zl == jnp.where(half == 0, NZ // 2, NZ // 2 - 1)
    far_above = zl >= jnp.where(half == 0, NZ // 2, NZ // 2 - 1)
    far_below = zl <= jnp.where(half == 0, NZ // 2, NZ // 2 - 1)

    @pl.when(far_target)
    def _():
        for x in range(NX):
            greet(at(dp_=other * NX + x, z_=dp))

    for k in PEERS_Y:
        greet(at(y_=y_peer(k)))
    for k in (2, 1, 3):
        greet(near(x_peer(k)))
    greet(sibling)

    up_half = jnp.where(zl < NZ - 1, half, other)
    dn_half = jnp.where(zl > 0, half, other)
    up = at(dp_=up_half * NX + px, z_=lax.rem(zl + 1, NZ))
    dn = at(dp_=dn_half * NX + px, z_=lax.rem(zl + NZ - 1, NZ))
    greet(up)
    greet(dn)

    for j in range(2 * NZ):
        pltpu.make_async_copy(weight_hbm.at[:, pl.ds(j * width, width)], weight.at[j], w_sem).start()

    contract_rows = (((0,), (0,)), ((), ()))

    expert_id = lax.broadcasted_iota(jnp.int32, (16, tokens), 0)
    first = routes_ref[0:1, :] == expert_id
    second = routes_ref[1:2, :] == expert_id
    named = jnp.where(first | second, 1.0, 0.0)
    gates = gates_ref[...].astype(F32)
    token_gate = jnp.where(first, gates[0:1, :], 0.0) + jnp.where(second, gates[1:2, :], 0.0)
    row = lax.broadcasted_iota(jnp.int32, (tokens, tokens), 0)
    col = lax.broadcasted_iota(jnp.int32, (tokens, tokens), 1)
    after = jnp.where(row < col, 1.0, 0.0).astype(BF16)
    earlier = jnp.dot(named.astype(BF16), after, preferred_element_type=F32)
    table = jnp.where(named > 0.5, earlier, -1.0)
    slot = lax.broadcasted_iota(jnp.int32, (CAP, tokens), 0).astype(F32)

    def build_place(table):
        for e in range(NE):
            hit = jnp.where(table[e:e + 1, :] == slot, 1.0, 0.0)
            place[e * CAP:(e + 1) * CAP, :] = hit.astype(BF16)

    for e in range(NE):
        hit = jnp.where(table[e:e + 1, :] == slot, 1.0, 0.0)
        place[e * CAP:(e + 1) * CAP, :] = hit.astype(BF16)
        gate = jnp.sum(hit * token_gate[e:e + 1, :], axis=1, keepdims=True)
        gate_out[e * CAP:(e + 1) * CAP, :] = jnp.broadcast_to(gate, (CAP, 128)).astype(BF16)

    gate_in[mine, :] = gate_out[mine, :]
    tok[zl] = grad_ref[...]
    far_src[0:tokens, :] = grad_ref[...]
    far_src[tokens:tokens + 16, 0:tokens] = table.astype(BF16)

    def pick(z):
        picked[z] = jnp.dot(place[...], tok[z], preferred_element_type=F32).astype(BF16)
        slots[z, core, mine, :] = picked[z, mine, :]

    def send_picked(z):
        for k in PEERS_Y:
            to = y_peer(k)
            there = pl.ds(pl.multiple_of(to * CAP, CAP), CAP)
            remote(picked.at[z, there], slots.at[z, core, mine], pick_s.at[z], pick_r.at[z], at(y_=to)).start()

    pick(zl)

    pl.semaphore_wait(barrier, 13 + jnp.where(far_source, 1, 0))

    for k in PEERS_Y:
        to = y_peer(k)
        there = pl.ds(pl.multiple_of(to * CAP, CAP), CAP)
        remote(gate_out.at[there], gate_in.at[mine], gate_s, gate_r, at(y_=to)).start()

    @pl.when(zl < NZ - 1)
    def _():
        remote(tok.at[zl], tok.at[zl], tok_up.at[zl], tok_r.at[zl], at(z_=zl + 1)).start()

    @pl.when(zl > 0)
    def _():
        remote(tok.at[zl], tok.at[zl], tok_dn.at[zl], tok_r.at[zl], at(z_=zl - 1)).start()

    @pl.when(far_source)
    def _():
        land = jnp.where(other == 0, NZ // 2, NZ // 2 - 1)
        remote(far_src, far_tok.at[px], far_s, far_r.at[px], at(dp_=zl, z_=land)).start()

    send_picked(zl)

    gate_pre = saved_ref[0].astype(F32)
    up_pre = saved_ref[1].astype(F32)
    sig = jax.nn.sigmoid(gate_pre)
    silu = gate_pre * sig
    fac_gate[...] = up_pre * sig * (1.0 + gate_pre * (1.0 - sig))
    fac_up[...] = silu
    act[...] = silu * up_pre

    def nearest(k):
        short = jnp.minimum(zl, NZ - 1 - zl)
        step = lax.div(k + 1, 2)
        zigzag = jnp.where(lax.rem(k, 2) == 1, zl - step, zl + step)
        return jnp.where(k <= 2 * short, zigzag, jnp.where(zl < NZ // 2, k, NZ - 1 - k))

    def pass_far(q, carry):
        block = far_tok.at[q]
        drain(block, far_r.at[q])

        @pl.when(far_above & (zl < NZ - 1))
        def _():
            remote(block, block, far_up.at[q], far_r.at[q], at(z_=zl + 1)).start()

        @pl.when(far_below & (zl > 0))
        def _():
            remote(block, block, far_dn.at[q], far_r.at[q], at(z_=zl - 1)).start()

        return carry

    part_rows = nslots // PARTS

    def part_of(where, h):
        return scaled.at[where, pl.ds(pl.multiple_of(h * part_rows, part_rows), part_rows)]

    def hop_to(q):
        return up if q < PARTS // 2 else dn

    def hop_first():
        for q in (0, 2, 1, 3):
            remote(part_of(dp, q), hop.at[0, q], hop_s.at[0, q], hop_r.at[0, q], hop_to(q)).start()

    def hop_on(d):
        for q in (0, 2, 1, 3):
            drain(hop.at[d - 1, q], hop_r.at[d - 1, q])
            remote(hop.at[d - 1, q], hop.at[d, q], hop_s.at[d, q], hop_r.at[d, q], hop_to(q)).start()

    def hop_last():
        d = NZ - 1
        for q in (0, 2, 1, 3):
            there = 1 - (up_half if q < PARTS // 2 else dn_half)
            drain(hop.at[d - 1, q], hop_r.at[d - 1, q])
            remote(
                hop.at[d - 1, q], part_of(there * NX + px, q), hop_s.at[d, q], hop_r.at[d, q], hop_to(q)
            ).start()

    far_step = 2 + jnp.abs(zl - jnp.where(half == 0, NZ // 2, NZ // 2 - 1))

    def pass_tokens(t, carry):
        below, above = zl - t, zl + t

        @pl.when(below >= 0)
        def _():
            block = tok.at[below]
            drain(block, tok_r.at[below])

            @pl.when(zl < NZ - 1)
            def _():
                remote(block, block, tok_up.at[below], tok_r.at[below], at(z_=zl + 1)).start()

        @pl.when(above < NZ)
        def _():
            block = tok.at[above]
            drain(block, tok_r.at[above])

            @pl.when(zl > 0)
            def _():
                remote(block, block, tok_dn.at[above], tok_r.at[above], at(z_=zl - 1)).start()

        @pl.when(below >= 0)
        def _():
            pick(below)
            send_picked(below)

        @pl.when(above < NZ)
        def _():
            pick(above)
            send_picked(above)

        @pl.when(t >= 2)
        def _():
            hop_on(t - 1)

        @pl.when(t == far_step)
        def _():
            lax.fori_loop(0, NX, pass_far, 0)

        return carry

    lax.fori_loop(1, 2, pass_tokens, 0)

    drain(gate_in.at[0:nslots - CAP], gate_r)
    gate_col = gate_in[...].astype(F32)[:, 0:1]
    scaled[dp] = (gate_col * act[...]).astype(BF16)
    for k in (2, 1, 3):
        x = x_peer(k)
        remote(scaled.at[dp], scaled.at[dp], sc_s.at[x], sc_r.at[px], near(x)).start()

    hop_first()
    lax.fori_loop(2, NZ, pass_tokens, 0)
    hop_last()

    drain(weight, w_sem)
    raw[...] = jnp.zeros_like(raw)
    total[...] = jnp.zeros_like(total)

    def add_raw(z, c):
        raw[...] += lax.dot_general(
            slots[z, c], weight[2 * z + c], (((1,), (1,)), ((), ())), preferred_element_type=F32
        )

    def take_slots(k, carry):
        z = nearest(k)
        drain(slots.at[z, core, pl.ds(0, nslots - CAP)], pick_r.at[z])
        block = slots.at[z, core]
        remote(block, block, sib_s.at[z], sib_r.at[z], sibling).start()

        @pl.when((lax.div(z, NX) == half) & (z != dp))
        def _():
            x = lax.rem(z, NX)
            remote(block, rows.at[dp, core], near_s.at[x], near_r.at[px], near(x)).start()

        add_raw(z, core)

        @pl.when(k > 0)
        def _():
            before = nearest(jnp.maximum(k - 1, 0))
            drain(slots.at[before, 1 - core], sib_r.at[before])
            add_raw(before, 1 - core)

        return carry

    def take_far(q, carry):
        build_place(far_tok[q, tokens:tokens + 16, 0:tokens].astype(F32))
        far_picked[q] = jnp.dot(
            place[...], far_tok[q, 0:tokens, :], preferred_element_type=F32
        ).astype(BF16)
        far_dp = other * NX + q
        rows[far_dp, core, mine, :] = far_picked[q, mine, :]
        for k in PEERS_Y:
            to = y_peer(k)
            there = pl.ds(pl.multiple_of(to * CAP, CAP), CAP)
            remote(
                far_picked.at[q, there], rows.at[far_dp, core, mine], fpick_s.at[q], fpick_r.at[q], at(y_=to)
            ).start()
        return carry

    lax.fori_loop(0, NX, take_far, 0)
    lax.fori_loop(0, 4, take_slots, 0)

    twin = other * NX + px

    def pass_part(q):
        part = part_of(twin, q)
        drain(part, hop_r.at[NZ - 1, q])
        for k in (2, 1, 3):
            x = x_peer(k)
            remote(part, part, fsc_s.at[x], fsc_r.at[px], near(x)).start()

    for q in (0, 2, 1, 3):
        pass_part(q)

    lax.fori_loop(4, NZ, take_slots, 0)
    last = nearest(NZ - 1)
    drain(slots.at[last, 1 - core], sib_r.at[last])
    add_raw(last, 1 - core)
    gated = gate_in[...].astype(F32)[:, 0:1] * raw[...]
    hidden_ref[0] = (gated * fac_gate[...]).astype(BF16)
    hidden_ref[1] = (gated * fac_up[...]).astype(BF16)

    def add_total(c, left, right):
        total[c] += lax.dot_general(left, right, contract_rows, preferred_element_type=F32)

    for c in range(2):
        add_total(c, slots[dp, c], scaled[dp])

    def near_arrive(k, carry):
        x = x_peer(k)
        src = half * NX + x
        block = rows.at[src, core]
        drain(block, near_r.at[x])
        remote(block, block, nsib_s.at[x], nsib_r.at[x], sibling).start()
        return carry

    lax.fori_loop(1, NX, near_arrive, 0)

    def near_add(k, carry):
        x = x_peer(k)
        src = half * NX + x
        drain(scaled.at[src], sc_r.at[x])
        add_total(core, rows[src, core], scaled[src])
        drain(rows.at[src, 1 - core], nsib_r.at[x])
        add_total(1 - core, rows[src, 1 - core], scaled[src])
        return carry

    lax.fori_loop(1, NX, near_add, 0)

    def far_arrive(q, carry):
        src = other * NX + q
        drain(rows.at[src, core, pl.ds(0, nslots - CAP)], fpick_r.at[q])
        block = rows.at[src, core]
        remote(block, block, fsib_s.at[q], fsib_r.at[q], sibling).start()
        return carry

    def far_add(q, carry):
        src = other * NX + q

        @pl.when(q != px)
        def _():
            drain(scaled.at[src], fsc_r.at[q])

        add_total(core, rows[src, core], scaled[src])
        drain(rows.at[src, 1 - core], fsib_r.at[q])
        add_total(1 - core, rows[src, 1 - core], scaled[src])
        return carry

    lax.fori_loop(0, NX, far_arrive, 0)
    lax.fori_loop(0, NX, far_add, 0)
    wgrad_ref[0:width, :] = total[0].astype(BF16)
    wgrad_ref[width:2 * width, :] = total[1].astype(BF16)

    drain(gate_out.at[0:nslots - CAP], gate_s)

    @pl.when(far_source)
    def _():
        drain(far_src, far_s)

    def sent_blocks(z, carry):
        @pl.when((z <= zl) & (zl < NZ - 1))
        def _():
            drain(tok.at[z], tok_up.at[z])

        @pl.when((z >= zl) & (zl > 0))
        def _():
            drain(tok.at[z], tok_dn.at[z])

        drain(picked.at[z, pl.ds(0, nslots - CAP)], pick_s.at[z])
        drain(slots.at[z, core], sib_s.at[z])
        return carry

    lax.fori_loop(0, NZ, sent_blocks, 0)

    def sent_parts(q, carry):
        @pl.when(far_above & (zl < NZ - 1))
        def _():
            drain(far_tok.at[q], far_up.at[q])

        @pl.when(far_below & (zl > 0))
        def _():
            drain(far_tok.at[q], far_dn.at[q])

        drain(far_picked.at[q, pl.ds(0, nslots - CAP)], fpick_s.at[q])
        drain(rows.at[q, core], fsib_s.at[q])

        @pl.when(q != px)
        def _():
            drain(rows.at[q, core], near_s.at[q])
            drain(rows.at[q, core], nsib_s.at[q])
            drain(scaled.at[q], sc_s.at[q])
            drain(scaled.at[q], fsc_s.at[q])

        return carry

    lax.fori_loop(0, NX, sent_parts, 0)

    def sent_hops(d, carry):
        for q in range(PARTS):
            drain(hop.at[0, q], hop_s.at[d, q])
        return carry

    lax.fori_loop(0, NZ, sent_hops, 0)


def hand_over(hidden_in, wgrad_in, hidden_out, wgrad_out):
    hidden_out[...] = hidden_in[...]
    wgrad_out[...] = wgrad_in[...]


def per_device(grad_out, routes, gate_weights, saved_hidden, down_weight):
    tokens, width = grad_out.shape
    nslots, units = saved_hidden.shape[3:]
    dma = pltpu.SemaphoreType.DMA
    vmem = pl.BlockSpec(memory_space=pltpu.VMEM)
    hidden_grad, weight_grad = pl.pallas_call(
        kernel,
        out_shape=(
            jax.ShapeDtypeStruct((2, nslots, units), BF16),
            jax.ShapeDtypeStruct((2 * width, units), BF16),
        ),
        in_specs=[vmem, vmem, vmem, vmem, pl.BlockSpec(memory_space=pl.ANY)],
        out_specs=(vmem, vmem),
        scratch_shapes=[
            pltpu.VMEM((NZ, tokens, width), BF16),
            pltpu.VMEM((nslots, tokens), BF16),
            pltpu.VMEM((tokens + 16, width), BF16),
            pltpu.VMEM((NZ, nslots, width), BF16),
            pltpu.VMEM((NZ, 2, nslots, width), BF16),
            pltpu.VMEM((nslots, 128), BF16),
            pltpu.VMEM((nslots, 128), BF16),
            pltpu.VMEM((2 * NZ, units, width), BF16),
            pltpu.VMEM((nslots, units), F32),
            pltpu.VMEM((nslots, units), F32),
            pltpu.VMEM((nslots, units), F32),
            pltpu.VMEM((nslots, units), F32),
            pltpu.VMEM((2 * NX, nslots, units), BF16),
            pltpu.VMEM((NZ - 1, PARTS, nslots // PARTS, units), BF16),
            pltpu.VMEM((NX, tokens + 16, width), BF16),
            pltpu.VMEM((NX, nslots, width), BF16),
            pltpu.VMEM((2 * NX, 2, nslots, width), BF16),
            pltpu.VMEM((2, width, units), F32),
            dma(()),
            dma(()), dma(()),
            dma((NZ,)), dma((NZ,)), dma((NZ,)),
            dma(()), dma((NX,)), dma((NX,)), dma((NX,)),
            dma((NZ,)), dma((NZ,)),
            dma((NZ,)), dma((NZ,)),
            dma((NX,)), dma((NX,)),
            dma((NX,)), dma((NX,)),
            dma((NX,)), dma((NX,)),
            dma((NX,)), dma((NX,)),
            dma((NZ, PARTS)), dma((NZ, PARTS)),
            dma((NX,)), dma((NX,)), dma((NX,)), dma((NX,)),
        ],
        compiler_params=pltpu.CompilerParams(
            collective_id=0, has_side_effects=True, vmem_limit_bytes=56 * 2**20
        ),
        name="moe_backward",
    )(grad_out, routes.T, gate_weights.T, saved_hidden[0, 0], down_weight[0])
    hidden_grad, weight_grad = pl.pallas_call(
        hand_over,
        out_shape=(
            jax.ShapeDtypeStruct(hidden_grad.shape, BF16),
            jax.ShapeDtypeStruct(weight_grad.shape, BF16),
        ),
        in_specs=[vmem, vmem],
        out_specs=(vmem, vmem),
        name="hand_over",
    )(hidden_grad, weight_grad)
    return hidden_grad[None, None], weight_grad[None]


def solution(mesh):
    placed = (
        P(("dp", "expert"), "etp"),
        P(("dp", "expert"), None),
        P(("dp", "expert"), None),
        P("dp", "expert", None, None, "etp"),
        P("expert", "etp", None),
    )
    return jax.shard_map(
        per_device,
        mesh=mesh,
        in_specs=placed,
        out_specs=(P("dp", "expert", None, None, "etp"), P("expert", "dp", "etp")),
        check_vma=False,
    )
```

```python
import jax
import jax.numpy as jnp
from jax import lax
from jax.experimental import pallas as pl
from jax.experimental.pallas import tpu as pltpu
from jax.sharding import PartitionSpec as P

MESH = pl.DeviceIdType.MESH
BF16 = jnp.bfloat16
F32 = jnp.float32
NE = 8
NX = 4
NZ = 8
CAP = 32
PARTS = 4
PEERS_Y = (4, 3, 5, 2, 6, 1, 7)


def kernel(
    grad_ref, routes_ref, gates_ref, saved_ref, weight_hbm, hidden_ref, wgrad_ref,
    tok, place, far_src, picked, slots, gate_out, gate_in, weight, raw, fac_gate, fac_up, act,
    scaled, hop, far_tok, far_picked, rows, total,
    w_sem, gate_s, gate_r, tok_up, tok_dn, tok_r, far_s, far_r, far_up, far_dn, pick_s, pick_r,
    sib_s, sib_r, near_s, near_r, nsib_s, nsib_r, fpick_s, fpick_r, fsib_s, fsib_r,
    hop_s, hop_r, sc_s, sc_r, fsc_s, fsc_r,
):
    dp = lax.axis_index("dp")
    y = lax.axis_index("expert")
    etp = lax.axis_index("etp")
    half, px = lax.div(dp, NX), lax.rem(dp, NX)
    zl, core = lax.div(etp, 2), lax.rem(etp, 2)
    other = 1 - half
    tokens, width = grad_ref.shape
    nslots = NE * CAP
    mine = pl.ds(pl.multiple_of(y * CAP, CAP), CAP)

    def at(dp_=None, y_=None, z_=None, core_=None):
        return {
            "dp": dp if dp_ is None else dp_,
            "expert": y if y_ is None else y_,
            "etp": (zl if z_ is None else z_) * 2 + (core if core_ is None else core_),
        }

    def y_peer(k):
        return lax.rem(y + k, NE)

    def x_peer(k):
        return lax.rem(px + k, NX)

    def near(x):
        return at(dp_=half * NX + x)

    sibling = at(core_=1 - core)

    def remote(src, dst, send, recv, where):
        return pltpu.make_async_remote_copy(
            src_ref=src, dst_ref=dst, send_sem=send, recv_sem=recv, device_id=where, device_id_type=MESH
        )

    def drain(ref, sem):
        pltpu.make_async_copy(ref, ref, sem).wait()

    barrier = pltpu.get_barrier_semaphore()

    def greet(where):
        pl.semaphore_signal(barrier, inc=1, device_id=where, device_id_type=MESH)

    far_source = lax.div(zl, NX) == other
    far_target = zl == jnp.where(half == 0, NZ // 2, NZ // 2 - 1)
    far_above = zl >= jnp.where(half == 0, NZ // 2, NZ // 2 - 1)
    far_below = zl <= jnp.where(half == 0, NZ // 2, NZ // 2 - 1)

    @pl.when(far_target)
    def _():
        for x in range(NX):
            greet(at(dp_=other * NX + x, z_=dp))

    for k in PEERS_Y:
        greet(at(y_=y_peer(k)))
    for k in (2, 1, 3):
        greet(near(x_peer(k)))
    greet(sibling)

    up_half = jnp.where(zl < NZ - 1, half, other)
    dn_half = jnp.where(zl > 0, half, other)
    up = at(dp_=up_half * NX + px, z_=lax.rem(zl + 1, NZ))
    dn = at(dp_=dn_half * NX + px, z_=lax.rem(zl + NZ - 1, NZ))
    greet(up)
    greet(dn)

    for j in range(2 * NZ):
        pltpu.make_async_copy(weight_hbm.at[:, pl.ds(j * width, width)], weight.at[j], w_sem).start()

    contract_rows = (((0,), (0,)), ((), ()))

    expert_id = lax.broadcasted_iota(jnp.int32, (16, tokens), 0)
    first = routes_ref[0:1, :] == expert_id
    second = routes_ref[1:2, :] == expert_id
    named = jnp.where(first | second, 1.0, 0.0)
    gates = gates_ref[...].astype(F32)
    token_gate = jnp.where(first, gates[0:1, :], 0.0) + jnp.where(second, gates[1:2, :], 0.0)
    row = lax.broadcasted_iota(jnp.int32, (tokens, tokens), 0)
    col = lax.broadcasted_iota(jnp.int32, (tokens, tokens), 1)
    after = jnp.where(row < col, 1.0, 0.0).astype(BF16)
    earlier = jnp.dot(named.astype(BF16), after, preferred_element_type=F32)
    table = jnp.where(named > 0.5, earlier, -1.0)
    slot = lax.broadcasted_iota(jnp.int32, (CAP, tokens), 0).astype(F32)

    def build_place(table):
        for e in range(NE):
            hit = jnp.where(table[e:e + 1, :] == slot, 1.0, 0.0)
            place[e * CAP:(e + 1) * CAP, :] = hit.astype(BF16)

    for e in range(NE):
        hit = jnp.where(table[e:e + 1, :] == slot, 1.0, 0.0)
        place[e * CAP:(e + 1) * CAP, :] = hit.astype(BF16)
        gate = jnp.sum(hit * token_gate[e:e + 1, :], axis=1, keepdims=True)
        gate_out[e * CAP:(e + 1) * CAP, :] = jnp.broadcast_to(gate, (CAP, 128)).astype(BF16)

    gate_in[mine, :] = gate_out[mine, :]
    tok[zl] = grad_ref[...]
    far_src[0:tokens, :] = grad_ref[...]
    far_src[tokens:tokens + 16, 0:tokens] = table.astype(BF16)

    def pick(z):
        picked[z] = jnp.dot(place[...], tok[z], preferred_element_type=F32).astype(BF16)
        slots[z, core, mine, :] = picked[z, mine, :]

    def send_picked(z):
        for k in PEERS_Y:
            to = y_peer(k)
            there = pl.ds(pl.multiple_of(to * CAP, CAP), CAP)
            remote(picked.at[z, there], slots.at[z, core, mine], pick_s.at[z], pick_r.at[z], at(y_=to)).start()

    pick(zl)

    pl.semaphore_wait(barrier, 13 + jnp.where(far_source, 1, 0))

    for k in PEERS_Y:
        to = y_peer(k)
        there = pl.ds(pl.multiple_of(to * CAP, CAP), CAP)
        remote(gate_out.at[there], gate_in.at[mine], gate_s, gate_r, at(y_=to)).start()

    @pl.when(zl < NZ - 1)
    def _():
        remote(tok.at[zl], tok.at[zl], tok_up.at[zl], tok_r.at[zl], at(z_=zl + 1)).start()

    @pl.when(zl > 0)
    def _():
        remote(tok.at[zl], tok.at[zl], tok_dn.at[zl], tok_r.at[zl], at(z_=zl - 1)).start()

    @pl.when(far_source)
    def _():
        land = jnp.where(other == 0, NZ // 2, NZ // 2 - 1)
        remote(far_src, far_tok.at[px], far_s, far_r.at[px], at(dp_=zl, z_=land)).start()

    send_picked(zl)

    gate_pre = saved_ref[0].astype(F32)
    up_pre = saved_ref[1].astype(F32)
    sig = jax.nn.sigmoid(gate_pre)
    silu = gate_pre * sig
    fac_gate[...] = up_pre * sig * (1.0 + gate_pre * (1.0 - sig))
    fac_up[...] = silu
    act[...] = silu * up_pre

    def nearest(k):
        short = jnp.minimum(zl, NZ - 1 - zl)
        step = lax.div(k + 1, 2)
        zigzag = jnp.where(lax.rem(k, 2) == 1, zl - step, zl + step)
        return jnp.where(k <= 2 * short, zigzag, jnp.where(zl < NZ // 2, k, NZ - 1 - k))

    def pass_far(q, carry):
        block = far_tok.at[q]
        drain(block, far_r.at[q])

        @pl.when(far_above & (zl < NZ - 1))
        def _():
            remote(block, block, far_up.at[q], far_r.at[q], at(z_=zl + 1)).start()

        @pl.when(far_below & (zl > 0))
        def _():
            remote(block, block, far_dn.at[q], far_r.at[q], at(z_=zl - 1)).start()

        return carry

    part_rows = nslots // PARTS

    def part_of(where, h):
        return scaled.at[where, pl.ds(pl.multiple_of(h * part_rows, part_rows), part_rows)]

    def hop_to(q):
        return up if q < PARTS // 2 else dn

    def hop_first():
        for q in (0, 2, 1, 3):
            remote(part_of(dp, q), hop.at[0, q], hop_s.at[0, q], hop_r.at[0, q], hop_to(q)).start()

    def hop_on(d):
        for q in (0, 2, 1, 3):
            drain(hop.at[d - 1, q], hop_r.at[d - 1, q])
            remote(hop.at[d - 1, q], hop.at[d, q], hop_s.at[d, q], hop_r.at[d, q], hop_to(q)).start()

    def hop_last():
        d = NZ - 1
        for q in (0, 2, 1, 3):
            there = 1 - (up_half if q < PARTS // 2 else dn_half)
            drain(hop.at[d - 1, q], hop_r.at[d - 1, q])
            remote(
                hop.at[d - 1, q], part_of(there * NX + px, q), hop_s.at[d, q], hop_r.at[d, q], hop_to(q)
            ).start()

    far_step = 2 + jnp.abs(zl - jnp.where(half == 0, NZ // 2, NZ // 2 - 1))

    def pass_tokens(t, carry):
        below, above = zl - t, zl + t

        @pl.when(below >= 0)
        def _():
            block = tok.at[below]
            drain(block, tok_r.at[below])

            @pl.when(zl < NZ - 1)
            def _():
                remote(block, block, tok_up.at[below], tok_r.at[below], at(z_=zl + 1)).start()

        @pl.when(above < NZ)
        def _():
            block = tok.at[above]
            drain(block, tok_r.at[above])

            @pl.when(zl > 0)
            def _():
                remote(block, block, tok_dn.at[above], tok_r.at[above], at(z_=zl - 1)).start()

        @pl.when(below >= 0)
        def _():
            pick(below)
            send_picked(below)

        @pl.when(above < NZ)
        def _():
            pick(above)
            send_picked(above)

        @pl.when(t >= 2)
        def _():
            hop_on(t - 1)

        @pl.when(t == far_step)
        def _():
            lax.fori_loop(0, NX, pass_far, 0)

        return carry

    lax.fori_loop(1, 2, pass_tokens, 0)

    drain(gate_in.at[0:nslots - CAP], gate_r)
    gate_col = gate_in[...].astype(F32)[:, 0:1]
    scaled[dp] = (gate_col * act[...]).astype(BF16)
    for k in (2, 1, 3):
        x = x_peer(k)
        remote(scaled.at[dp], scaled.at[dp], sc_s.at[x], sc_r.at[px], near(x)).start()

    hop_first()
    lax.fori_loop(2, NZ, pass_tokens, 0)
    hop_last()

    drain(weight, w_sem)
    raw[...] = jnp.zeros_like(raw)
    total[...] = jnp.zeros_like(total)

    def add_raw(z, c):
        raw[...] += lax.dot_general(
            slots[z, c], weight[2 * z + c], (((1,), (1,)), ((), ())), preferred_element_type=F32
        )

    def take_slots(k, carry):
        z = nearest(k)
        drain(slots.at[z, core, pl.ds(0, nslots - CAP)], pick_r.at[z])
        block = slots.at[z, core]
        remote(block, block, sib_s.at[z], sib_r.at[z], sibling).start()

        @pl.when((lax.div(z, NX) == half) & (z != dp))
        def _():
            x = lax.rem(z, NX)
            remote(block, rows.at[dp, core], near_s.at[x], near_r.at[px], near(x)).start()

        add_raw(z, core)

        @pl.when(k > 0)
        def _():
            before = nearest(jnp.maximum(k - 1, 0))
            drain(slots.at[before, 1 - core], sib_r.at[before])
            add_raw(before, 1 - core)

        return carry

    def take_far(q, carry):
        build_place(far_tok[q, tokens:tokens + 16, 0:tokens].astype(F32))
        far_picked[q] = jnp.dot(
            place[...], far_tok[q, 0:tokens, :], preferred_element_type=F32
        ).astype(BF16)
        far_dp = other * NX + q
        rows[far_dp, core, mine, :] = far_picked[q, mine, :]
        for k in PEERS_Y:
            to = y_peer(k)
            there = pl.ds(pl.multiple_of(to * CAP, CAP), CAP)
            remote(
                far_picked.at[q, there], rows.at[far_dp, core, mine], fpick_s.at[q], fpick_r.at[q], at(y_=to)
            ).start()
        return carry

    lax.fori_loop(0, NX, take_far, 0)
    lax.fori_loop(0, 6, take_slots, 0)

    twin = other * NX + px

    def pass_part(q):
        part = part_of(twin, q)
        drain(part, hop_r.at[NZ - 1, q])
        for k in (2, 1, 3):
            x = x_peer(k)
            remote(part, part, fsc_s.at[x], fsc_r.at[px], near(x)).start()

    for q in (0, 2, 1, 3):
        pass_part(q)

    lax.fori_loop(6, NZ, take_slots, 0)
    last = nearest(NZ - 1)
    drain(slots.at[last, 1 - core], sib_r.at[last])
    add_raw(last, 1 - core)
    def near_arrive(k, carry):
        x = x_peer(k)
        src = half * NX + x
        block = rows.at[src, core]
        drain(block, near_r.at[x])
        remote(block, block, nsib_s.at[x], nsib_r.at[x], sibling).start()
        return carry

    lax.fori_loop(1, NX, near_arrive, 0)

    gated = gate_in[...].astype(F32)[:, 0:1] * raw[...]
    hidden_ref[0] = (gated * fac_gate[...]).astype(BF16)
    hidden_ref[1] = (gated * fac_up[...]).astype(BF16)

    def add_total(c, left, right):
        total[c] += lax.dot_general(left, right, contract_rows, preferred_element_type=F32)

    for c in range(2):
        add_total(c, slots[dp, c], scaled[dp])

    def near_add(k, carry):
        x = x_peer(k)
        src = half * NX + x
        drain(scaled.at[src], sc_r.at[x])
        add_total(core, rows[src, core], scaled[src])
        drain(rows.at[src, 1 - core], nsib_r.at[x])
        add_total(1 - core, rows[src, 1 - core], scaled[src])
        return carry

    lax.fori_loop(1, NX, near_add, 0)

    def far_arrive(q, carry):
        src = other * NX + q
        drain(rows.at[src, core, pl.ds(0, nslots - CAP)], fpick_r.at[q])
        block = rows.at[src, core]
        remote(block, block, fsib_s.at[q], fsib_r.at[q], sibling).start()
        return carry

    def far_add(q, carry):
        src = other * NX + q

        @pl.when(q != px)
        def _():
            drain(scaled.at[src], fsc_r.at[q])

        add_total(core, rows[src, core], scaled[src])
        drain(rows.at[src, 1 - core], fsib_r.at[q])
        add_total(1 - core, rows[src, 1 - core], scaled[src])
        return carry

    lax.fori_loop(0, NX, far_arrive, 0)
    lax.fori_loop(0, NX, far_add, 0)
    wgrad_ref[0:width, :] = total[0].astype(BF16)
    wgrad_ref[width:2 * width, :] = total[1].astype(BF16)

    drain(gate_out.at[0:nslots - CAP], gate_s)

    @pl.when(far_source)
    def _():
        drain(far_src, far_s)

    def sent_blocks(z, carry):
        @pl.when((z <= zl) & (zl < NZ - 1))
        def _():
            drain(tok.at[z], tok_up.at[z])

        @pl.when((z >= zl) & (zl > 0))
        def _():
            drain(tok.at[z], tok_dn.at[z])

        drain(picked.at[z, pl.ds(0, nslots - CAP)], pick_s.at[z])
        drain(slots.at[z, core], sib_s.at[z])
        return carry

    lax.fori_loop(0, NZ, sent_blocks, 0)

    def sent_parts(q, carry):
        @pl.when(far_above & (zl < NZ - 1))
        def _():
            drain(far_tok.at[q], far_up.at[q])

        @pl.when(far_below & (zl > 0))
        def _():
            drain(far_tok.at[q], far_dn.at[q])

        drain(far_picked.at[q, pl.ds(0, nslots - CAP)], fpick_s.at[q])
        drain(rows.at[q, core], fsib_s.at[q])

        @pl.when(q != px)
        def _():
            drain(rows.at[q, core], near_s.at[q])
            drain(rows.at[q, core], nsib_s.at[q])
            drain(scaled.at[q], sc_s.at[q])
            drain(scaled.at[q], fsc_s.at[q])

        return carry

    lax.fori_loop(0, NX, sent_parts, 0)

    def sent_hops(d, carry):
        for q in range(PARTS):
            drain(hop.at[0, q], hop_s.at[d, q])
        return carry

    lax.fori_loop(0, NZ, sent_hops, 0)


def hand_over(hidden_in, wgrad_in, hidden_out, wgrad_out):
    hidden_out[...] = hidden_in[...]
    wgrad_out[...] = wgrad_in[...]


def per_device(grad_out, routes, gate_weights, saved_hidden, down_weight):
    tokens, width = grad_out.shape
    nslots, units = saved_hidden.shape[3:]
    dma = pltpu.SemaphoreType.DMA
    vmem = pl.BlockSpec(memory_space=pltpu.VMEM)
    hidden_grad, weight_grad = pl.pallas_call(
        kernel,
        out_shape=(
            jax.ShapeDtypeStruct((2, nslots, units), BF16),
            jax.ShapeDtypeStruct((2 * width, units), BF16),
        ),
        in_specs=[vmem, vmem, vmem, vmem, pl.BlockSpec(memory_space=pl.ANY)],
        out_specs=(vmem, vmem),
        scratch_shapes=[
            pltpu.VMEM((NZ, tokens, width), BF16),
            pltpu.VMEM((nslots, tokens), BF16),
            pltpu.VMEM((tokens + 16, width), BF16),
            pltpu.VMEM((NZ, nslots, width), BF16),
            pltpu.VMEM((NZ, 2, nslots, width), BF16),
            pltpu.VMEM((nslots, 128), BF16),
            pltpu.VMEM((nslots, 128), BF16),
            pltpu.VMEM((2 * NZ, units, width), BF16),
            pltpu.VMEM((nslots, units), F32),
            pltpu.VMEM((nslots, units), F32),
            pltpu.VMEM((nslots, units), F32),
            pltpu.VMEM((nslots, units), F32),
            pltpu.VMEM((2 * NX, nslots, units), BF16),
            pltpu.VMEM((NZ - 1, PARTS, nslots // PARTS, units), BF16),
            pltpu.VMEM((NX, tokens + 16, width), BF16),
            pltpu.VMEM((NX, nslots, width), BF16),
            pltpu.VMEM((2 * NX, 2, nslots, width), BF16),
            pltpu.VMEM((2, width, units), F32),
            dma(()),
            dma(()), dma(()),
            dma((NZ,)), dma((NZ,)), dma((NZ,)),
            dma(()), dma((NX,)), dma((NX,)), dma((NX,)),
            dma((NZ,)), dma((NZ,)),
            dma((NZ,)), dma((NZ,)),
            dma((NX,)), dma((NX,)),
            dma((NX,)), dma((NX,)),
            dma((NX,)), dma((NX,)),
            dma((NX,)), dma((NX,)),
            dma((NZ, PARTS)), dma((NZ, PARTS)),
            dma((NX,)), dma((NX,)), dma((NX,)), dma((NX,)),
        ],
        compiler_params=pltpu.CompilerParams(
            collective_id=0, has_side_effects=True, vmem_limit_bytes=56 * 2**20
        ),
        name="moe_backward",
    )(grad_out, routes.T, gate_weights.T, saved_hidden[0, 0], down_weight[0])
    hidden_grad, weight_grad = pl.pallas_call(
        hand_over,
        out_shape=(
            jax.ShapeDtypeStruct(hidden_grad.shape, BF16),
            jax.ShapeDtypeStruct(weight_grad.shape, BF16),
        ),
        in_specs=[vmem, vmem],
        out_specs=(vmem, vmem),
        name="hand_over",
    )(hidden_grad, weight_grad)
    return hidden_grad[None, None], weight_grad[None]


def solution(mesh):
    placed = (
        P(("dp", "expert"), "etp"),
        P(("dp", "expert"), None),
        P(("dp", "expert"), None),
        P("dp", "expert", None, None, "etp"),
        P("expert", "etp", None),
    )
    return jax.shard_map(
        per_device,
        mesh=mesh,
        in_specs=placed,
        out_specs=(P("dp", "expert", None, None, "etp"), P("expert", "dp", "etp")),
        check_vma=False,
    )
```
